32 devices in a mesh: sub: 16 (over z, y, x), panel: 2 (over core).
Axes of the slice: x: 2, y: 2, z: 4, core: 2. Of those that a mesh axis runs over, the one named last changes fastest.
Arguments:
- stiffness_tiles: bfloat16 [256, 8, 128, 128], P('sub'), may hold values from -0.1875 to 0.1875
- tile_columns: int32 [256, 8], P('sub'), may hold values from 0 to 19
- tile_counts: int32 [16, 16], P('sub'), may hold values from 1 to 8, 96 in all within a row
- phi_modes: bfloat16 [32768, 2048], P('sub', 'panel'), may hold values from -1.5 to 1.5
- halo_to_right: int32 [32], P('sub'), may hold values from 0 to 15
- halo_to_left: int32 [32], P('sub'), may hold values from 0 to 15
- liner_rows: int32 [8192], P('sub'), may hold values from 0 to 2047
- liner_owner: int32 [8192, 1], P('sub'), may hold values from 0 to 15; in each aligned block of 512 rows (0 to 511, 512 to 1023, ...) at most 32 rows name the same one
- liner_slot: int32 [8192], P('sub'), may hold values from 0 to 31
Outputs:
- reduced: float32 [2048, 2048], P('sub', 'panel')
- interface_load: float32 [512, 2048], P('sub', 'panel')
The draws below stay inside these ranges and needn't reach their ends.
Inputs may be any that keep to these rules, and one draw needn't show every extreme that they name: `tile_counts`: counts a slab's used slots; the counts of one slab sum to 96. `tile_columns`: indices into the slab's extended tiles. `liner_owner`: among the listed rows of one slab at most 32 name one owner, and in every draw some owner is named by exactly 32 rows of some slab.
All inputs are finite; a program needn't handle non-finite values.
Results may differ from the reference program's by a relative error of at most 0.0029.
Values may be sent and summed in bfloat16 or wider, within the bound.
A program may use at most 128 MiB of HBM per device.

```python
import math
import jax
import jax.numpy as jnp
import numpy as np
from jax import lax

MODES = 2048
TILE = 128
NNZ = 8
NBR = 16
HALO_T = 2
SEND_DEV = 512
CAP = 32
IF_DEV = 32
ROWS = 2048
DOFS = 32768
N_SUB = 16


def with_ends(result, stream_key, low, largest):
    index_at = [jax.random.randint(jax.random.fold_in(stream_key, axis), (), 0, length) for axis, length in enumerate(result.shape)]
    widest = result.shape.index(max(result.shape))
    beside = index_at[:widest] + [(index_at[widest] + 1) % result.shape[widest]] + index_at[widest + 1:]
    return result.at[tuple(index_at)].set(low).at[tuple(beside)].set(largest)


def with_spikes(values, key, source, target, blocks, factor):
    owner, partner = [(jnp.arange(values.shape[position]) // (values.shape[position] // blocks)).reshape([-1 if axis == position else 1 for axis in range(values.ndim)]) for position in (source, target)]
    chosen = jax.random.permutation(key, blocks)[partner]
    strong = (owner == chosen) | (owner == (partner + blocks // 2) % blocks)
    return jnp.where(strong, factor * values, values)


def block_scale(stream_key, dims, cuts, low, high):
    factor_of, own = 1.0, jax.random.fold_in(stream_key, 6)
    for dim, parts in cuts:
        steps = jnp.exp(jax.random.uniform(jax.random.fold_in(own, dim), (parts,), jnp.float32, low / len(cuts), high / len(cuts)))
        factor_of = factor_of * jnp.repeat(steps, dims[dim] // parts).reshape([-1 if axis == dim else 1 for axis in range(len(dims))])
    return factor_of


def split_up(number_of, total, bound, lean):
    loads = [(1 << 20) // math.isqrt(standing ** lean) + 1 for standing in range(2, number_of + 1)]
    rest, given = total - bound - (number_of - 1), [1] * (number_of - 1)
    while rest > 0:
        free = [i for i in range(number_of - 1) if given[i] < bound]
        mass, budget = sum([loads[i] for i in free]), rest
        for i in free:
            more = min(bound - given[i], max(1, budget * loads[i] // mass), rest)
            given[i] = given[i] + more
            rest = rest - more
    return np.array([bound] + given)


def uneven_parts(key, count, total, limit, skew):
    if count == 2:
        one = jax.random.randint(key, (), max(1, total - limit), min(limit, total - 1) + 1)
        return jnp.stack([one, total - one])
    sizes = jnp.asarray(split_up(count, total, limit, skew), jnp.int32)
    couples = (count - 1) // 2
    giver, sink = sizes[1:1 + 2 * couples:2], sizes[2:2 + 2 * couples:2]
    room = jnp.minimum(giver - 1, limit - sink)
    moved = jax.random.randint(jax.random.fold_in(key, 1), (couples,), 0, 1 << 20) % (room + 1)
    sizes = sizes.at[1:1 + 2 * couples:2].set(giver - moved).at[2:2 + 2 * couples:2].set(sink + moved)
    return sizes[jax.random.permutation(jax.random.fold_in(key, 2), count)]


def shared_out(own_key, own, number, rows, amount, top, bound, lean):
    ranking = jax.random.permutation(own_key, amount)
    crowded, usual = shares(amount, rows * top, bound, lean, True), shares(amount, rows * top, bound, lean, False)
    places = jnp.arange(amount)

    def named(tallies, turn):
        used = int((tallies > 0).sum())
        fixed = max(1, used // 4)
        moved = fixed + (places - fixed + turn * (used - fixed)) % max(1, amount - fixed)
        return jnp.zeros((amount,), jnp.int32).at[ranking[jnp.where(places < fixed, places, moved)]].set(jnp.asarray(tallies, jnp.int32))

    tallies = jnp.where(number % 4 == 0, named(crowded, number // 4), named(usual, number - number // 4 - 1))
    mixed = jax.random.permutation(jax.random.fold_in(own, 3), amount)
    giver, receiver = mixed[0:amount // 2 * 2:2], mixed[1:amount // 2 * 2:2]
    room = jnp.minimum(tallies[giver] - 1, bound - tallies[receiver]) // 2
    room = jnp.where((giver == ranking[0]) | (receiver == ranking[0]) | (tallies[receiver] == 0), 0, jnp.maximum(room, 0))
    moved = jax.random.randint(jax.random.fold_in(own, 4), (amount // 2,), 0, 1 << 20) % (room + 1)
    tallies = tallies.at[giver].add(-moved).at[receiver].add(moved)
    labels = jnp.searchsorted(jnp.cumsum(tallies), jnp.arange(rows * top), side="right").astype(jnp.int32)
    table = labels.reshape(top, rows).T
    table = table[jax.random.permutation(jax.random.fold_in(own, 1), rows)]
    turn = jax.random.randint(jax.random.fold_in(own, 2), (rows, 1), 0, top)
    return jnp.take_along_axis(table, (jnp.arange(top)[None, :] + turn) % top, axis=1)


def shares(number_of, total, bound, slope, full):
    loads = [(1 << 20) // math.isqrt(standing ** slope) + 1 for standing in range(1, number_of + 1)]
    largest = bound if full else min(bound, max(-(-total // number_of), total * loads[0] // sum(loads)))
    least = 1 if total - largest >= number_of - 1 else 0
    given, spare = [largest] + [least] * (number_of - 1), total - largest - least * (number_of - 1)
    while spare > 0:
        movable = [i for i in range(1, number_of) if given[i] < largest] or [i for i in range(1, number_of) if given[i] < bound]
        pool, left = sum([loads[i] for i in movable]), spare
        for i in movable:
            more = min(bound - given[i], max(1, left * loads[i] // pool), spare)
            given[i] = given[i] + more
            spare = spare - more
    return np.array(given)


def centred(rng, dims, deviation, limit, pieces=(), kind=jnp.bfloat16):
    factor_of = block_scale(rng, dims, pieces, -0.22, 0.18) if pieces else 1.0
    array = jax.random.normal(rng, dims, jnp.float32) * deviation * factor_of
    return jnp.minimum(jnp.maximum(array, -limit), limit).astype(kind)


def noise_with(key, dims, scale, most, split, heavy, kind=jnp.bfloat16):
    entries = scale * jax.random.normal(key, dims, jnp.float32)
    if split:
        entries = entries * block_scale(key, dims, split, -0.22, 0.18)
    return jnp.clip(with_spikes(entries, jax.random.fold_in(key, 3), *heavy), -most, most).astype(kind)


def setup_inputs(seed: int = 0) -> dict:
    keys = jax.random.split(jax.random.key(seed), 10)
    stiffness_tiles = centred(keys[0], (N_SUB * NBR, NNZ, TILE, TILE), (NNZ * TILE) ** -0.5, 0.1875, ((0, 16),))
    tile_columns = with_ends(jax.random.randint(keys[1], (N_SUB * NBR, NNZ), 0, NBR + 2 * HALO_T), jax.random.fold_in(keys[1], 1), 0, (NBR + 2 * HALO_T) - 1).astype(jnp.int32)
    tile_counts = jax.vmap(lambda own: uneven_parts(own, NBR, NBR * NNZ * 3 // 4, NNZ, 2))(jax.random.split(keys[2], N_SUB)).reshape((N_SUB, NBR)).astype(jnp.int32)
    phi_modes = noise_with(keys[3], (DOFS, MODES), (DOFS ** -0.25), 1.5, ((0, 16), (1, 2)), (0, 1, 16, 2.0))
    halo_to_right = with_ends(jax.random.randint(keys[4], (N_SUB * HALO_T,), 0, NBR), jax.random.fold_in(keys[4], 1), 0, NBR - 1).astype(jnp.int32)
    halo_to_left = with_ends(jax.random.randint(keys[5], (N_SUB * HALO_T,), 0, NBR), jax.random.fold_in(keys[5], 1), 0, NBR - 1).astype(jnp.int32)
    liner_rows = with_ends(jax.random.randint(keys[6], (N_SUB * SEND_DEV,), 0, ROWS), jax.random.fold_in(keys[6], 1), 0, ROWS - 1).astype(jnp.int32)
    liner_owner_keys = jax.random.split(jax.random.fold_in(keys[7], 1), (N_SUB * SEND_DEV) // SEND_DEV)
    liner_owner_turns = jax.random.permutation(jax.random.fold_in(keys[7], 3), (N_SUB * SEND_DEV) // SEND_DEV)
    liner_owner = jax.vmap(lambda own, number: shared_out(jax.random.fold_in(keys[7], 2), own, number, SEND_DEV, N_SUB, 1, CAP, 2))(liner_owner_keys, liner_owner_turns).reshape((N_SUB * SEND_DEV, 1))
    liner_slot = with_ends(jax.random.randint(keys[8], (N_SUB * SEND_DEV,), 0, IF_DEV), jax.random.fold_in(keys[8], 1), 0, IF_DEV - 1).astype(jnp.int32)
    return {"stiffness_tiles": stiffness_tiles, "tile_columns": tile_columns, "tile_counts": tile_counts, "phi_modes": phi_modes, "halo_to_right": halo_to_right, "halo_to_left": halo_to_left, "liner_rows": liner_rows, "liner_owner": liner_owner, "liner_slot": liner_slot}


def slab_product(packed):
    tiles_here, columns_here, counts_here, extended = packed
    slots = jnp.arange(NNZ, dtype=jnp.int32)
    usable = (slots[None, :] < counts_here[:, None]).astype(jnp.bfloat16)
    masked = tiles_here * usable[:, :, None, None]
    chosen = extended[columns_here]
    return jnp.einsum("bjrc,bjcm->brm", masked.astype(jnp.float32), chosen.astype(jnp.float32))


def reference(stiffness_tiles, tile_columns, tile_counts, phi_modes, halo_to_right, halo_to_left, liner_rows, liner_owner, liner_slot):
    phi_tiles = phi_modes.reshape(N_SUB, NBR, TILE, MODES)
    right_lists = halo_to_right.reshape(N_SUB, HALO_T)
    left_lists = halo_to_left.reshape(N_SUB, HALO_T)
    picker = jax.vmap(lambda group, listed: group[listed])
    sent_right = picker(phi_tiles, right_lists)
    sent_left = picker(phi_tiles, left_lists)
    blanks = jnp.zeros((1, HALO_T, TILE, MODES), jnp.bfloat16)
    left_halo = jnp.concatenate([blanks, sent_right[:-1]], axis=0)
    right_halo = jnp.concatenate([sent_left[1:], blanks], axis=0)
    extended = jnp.concatenate([left_halo, phi_tiles, right_halo], axis=1)
    kphi = lax.map(slab_product, (stiffness_tiles.reshape(N_SUB, NBR, NNZ, TILE, TILE), tile_columns.reshape(N_SUB, NBR, NNZ), tile_counts, extended))
    kphi = kphi.astype(jnp.bfloat16).reshape(N_SUB * ROWS, MODES)
    reduced = jnp.dot(phi_modes.T, kphi, preferred_element_type=jnp.float32)
    source = (jnp.arange(N_SUB * SEND_DEV, dtype=jnp.int32) // SEND_DEV) * ROWS + liner_rows
    values = kphi[source].astype(jnp.float32)
    target = liner_owner[:, 0] * IF_DEV + liner_slot
    interface_load = jax.ops.segment_sum(values, target, num_segments=N_SUB * IF_DEV)
    return reduced, interface_load
```

```python
import functools

import jax
import jax.numpy as jnp
from jax import lax
from jax.experimental import pallas as pl
from jax.experimental.pallas import tpu as pltpu
from jax.sharding import PartitionSpec as P

IF_DEV = 32
LOW = 4
MESH = pl.DeviceIdType.MESH


def kernel(
    n_sub,
    n_panel,
    cols_ref,
    counts_ref,
    to_right_ref,
    to_left_ref,
    rows_ref,
    target_ref,
    tiles_hbm,
    phi_hbm,
    red_ref,
    load_ref,
    ext,
    tiles,
    onehot,
    lhs,
    kphi,
    part,
    halo_out,
    s1_out,
    s1_in,
    s2_out,
    s2_in,
    z_out,
    z_in,
    local_sem,
    halo_send,
    halo_recv,
    pan_send,
    pan_recv,
    s1_send,
    s1_recv,
    s2_send,
    s2_recv,
    z_send,
    z_recv,
):
    block_rows, slots, tile, _ = tiles.shape
    halo = halo_out.shape[1]
    rows = block_rows * tile
    width = kphi.shape[1]
    high = n_sub // LOW
    mode_rows = red_ref.shape[0]
    out_rows = mode_rows + IF_DEV
    per_panel = high // n_panel
    sub = lax.axis_index("sub")
    panel = lax.axis_index("panel")
    low, my_high = lax.rem(sub, LOW), sub // LOW
    bit0, bit1 = lax.rem(low, 2), low // 2
    swap = lax.rem(panel, 2)
    first_bit = (1 - swap) * bit0 + swap * bit1
    second_bit = (1 - swap) * bit1 + swap * bit0
    first_weight, second_weight = 1 + swap, 2 - swap
    first_peer = sub + (1 - 2 * first_bit) * first_weight
    second_peer = sub + (1 - 2 * second_bit) * second_weight

    phi_copy = pltpu.make_async_copy(
        phi_hbm, ext.at[pl.ds(halo, block_rows)], local_sem.at[0]
    )
    tile_copy = pltpu.make_async_copy(tiles_hbm, tiles, local_sem.at[1])
    phi_copy.start()
    tile_copy.start()
    phi_copy.wait()
    for i in range(halo):
        halo_out[0, i] = ext[halo + to_right_ref[i]]
        halo_out[1, i] = ext[halo + to_left_ref[i]]
    zero_tiles = jnp.zeros((halo, tile, width), ext.dtype)

    @pl.when(sub == 0)
    def _():
        ext[pl.ds(0, halo)] = zero_tiles

    @pl.when(sub == n_sub - 1)
    def _():
        ext[pl.ds(halo + block_rows, halo)] = zero_tiles

    barrier = pltpu.get_barrier_semaphore()

    def greet(place):
        pl.semaphore_signal(barrier, inc=1, device_id=place, device_id_type=MESH)

    greet({"sub": first_peer, "panel": panel})
    greet({"sub": second_peer, "panel": panel})

    @pl.when(sub > 0)
    def _():
        greet({"sub": sub - 1, "panel": panel})

    @pl.when(sub < n_sub - 1)
    def _():
        greet({"sub": sub + 1, "panel": panel})

    for step in range(1, n_panel):
        greet({"sub": sub, "panel": lax.rem(panel + step, n_panel)})
    for step in range(1, high):
        greet({"sub": lax.rem(my_high + step, high) * LOW + low, "panel": panel})
    ends = jnp.where(sub > 0, 1, 0) + jnp.where(sub < n_sub - 1, 1, 0)
    pl.semaphore_wait(barrier, 2 + (n_panel - 1) + (high - 1) + ends)

    def halo_copy(side):
        return pltpu.make_async_remote_copy(
            src_ref=halo_out.at[side],
            dst_ref=ext.at[pl.ds(side * (halo + block_rows), halo)],
            send_sem=halo_send.at[side],
            recv_sem=halo_recv.at[side],
            device_id={"sub": sub + 1 - 2 * side, "panel": panel},
            device_id_type=MESH,
        )

    @pl.when(sub < n_sub - 1)
    def _():
        halo_copy(0).start()

    @pl.when(sub > 0)
    def _():
        halo_copy(1).start()

    def transposed(b, carry):
        for q in range(per_panel * LOW):
            lhs[
                panel * per_panel + q // LOW,
                q % LOW,
                pl.ds(0, mode_rows),
                pl.ds(pl.multiple_of(b * tile, tile), tile),
            ] = jnp.transpose(ext[halo + b, :, pl.ds(q * mode_rows, mode_rows)])
        return carry

    lax.fori_loop(0, block_rows, transposed, 0)

    def panel_copy(step, owner):
        block = lhs.at[
            pl.ds(owner * per_panel, per_panel), :, pl.ds(0, mode_rows), :
        ]
        return pltpu.make_async_remote_copy(
            src_ref=block,
            dst_ref=block,
            send_sem=pan_send.at[step],
            recv_sem=pan_recv.at[step],
            device_id={"sub": sub, "panel": lax.rem(panel + step, n_panel)},
            device_id_type=MESH,
        )

    for step in range(1, n_panel):
        panel_copy(step, panel).start()

    listed = rows_ref.shape[1]
    onehot[...] = (
        lax.broadcasted_iota(jnp.int32, (rows, listed), 0) == rows_ref[...]
    ).astype(jnp.float32).astype(jnp.bfloat16)
    wanted = LOW * IF_DEV

    def select(h, carry):
        place = lax.broadcasted_iota(jnp.int32, (wanted, listed), 0) + h * wanted
        hit = (place == target_ref[...]).astype(jnp.float32).astype(jnp.bfloat16)
        found = lax.dot_general(
            hit,
            onehot[...],
            (((1,), (1,)), ((), ())),
            preferred_element_type=jnp.float32,
        ).astype(jnp.bfloat16)
        for q in range(LOW):
            lhs[h, q, pl.ds(mode_rows, IF_DEV), :] = found[
                q * IF_DEV : (q + 1) * IF_DEV
            ]
        return carry

    lax.fori_loop(0, high, select, 0)
    tile_copy.wait()

    @pl.when(sub > 0)
    def _():
        halo_copy(0).wait_recv()

    @pl.when(sub < n_sub - 1)
    def _():
        halo_copy(1).wait_recv()

    def block_row(b, carry):
        count = counts_ref[0, b]
        left = jnp.concatenate(
            [
                jnp.where(j < count, tiles[b, j].astype(jnp.float32), 0.0).astype(
                    jnp.bfloat16
                )
                for j in range(slots)
            ],
            axis=1,
        )
        right = jnp.concatenate([ext[cols_ref[b, j]] for j in range(slots)], axis=0)
        kphi[pl.ds(pl.multiple_of(b * tile, tile), tile), :] = jnp.dot(
            left, right, preferred_element_type=jnp.float32
        ).astype(jnp.bfloat16)
        return carry

    lax.fori_loop(0, block_rows, block_row, 0)

    for step in range(1, n_panel):
        panel_copy(step, lax.rem(panel + n_panel - step, n_panel)).wait_recv()

    def first_copy(k):
        return pltpu.make_async_remote_copy(
            src_ref=s1_out.at[k],
            dst_ref=s1_in.at[k],
            send_sem=s1_send.at[k],
            recv_sem=s1_recv.at[k],
            device_id={"sub": first_peer, "panel": panel},
            device_id_type=MESH,
        )

    def second_copy(k):
        return pltpu.make_async_remote_copy(
            src_ref=s2_out.at[k],
            dst_ref=s2_in.at[k],
            send_sem=s2_send.at[k],
            recv_sem=s2_recv.at[k],
            device_id={"sub": second_peer, "panel": panel},
            device_id_type=MESH,
        )

    def third_copy(k, slot):
        return pltpu.make_async_remote_copy(
            src_ref=z_out.at[k],
            dst_ref=z_in.at[slot],
            send_sem=z_send.at[k],
            recv_sem=z_recv.at[slot],
            device_id={"sub": lax.rem(my_high + 1 + k, high) * LOW + low, "panel": panel},
            device_id_type=MESH,
        )

    chunk = min(256, width)

    def step_of(t, carry):
        @pl.when(t < high)
        def _():
            h = lax.rem(my_high + 1 + t, high)

            def columns(c, inner):
                at = pl.ds(pl.multiple_of(c * chunk, chunk), chunk)
                product = jnp.dot(
                    lhs[h].reshape(LOW * out_rows, rows),
                    kphi[:, at],
                    preferred_element_type=jnp.float32,
                )
                part[t, :, :, at] = product.reshape(LOW, out_rows, chunk)
                return inner

            lax.fori_loop(0, width // chunk, columns, 0)
            for j in range(2):
                q = (1 - first_bit) * first_weight + j * second_weight
                s1_out[t, j] = part[t, q].astype(jnp.bfloat16)
            first_copy(t).start()

        @pl.when((t >= 1) & (t < high + 1))
        def _():
            k = t - 1
            first_copy(k).wait_recv()
            q = first_bit * first_weight + (1 - second_bit) * second_weight
            s2_out[k] = (
                part[k, q] + s1_in[k, 1 - second_bit].astype(jnp.float32)
            ).astype(jnp.bfloat16)
            second_copy(k).start()

        @pl.when(t >= 2)
        def _():
            k = t - 2
            second_copy(k).wait_recv()
            total = (
                part[k, low]
                + s1_in[k, second_bit].astype(jnp.float32)
                + s2_in[k].astype(jnp.float32)
            )

            @pl.when(k < high - 1)
            def _():
                z_out[k] = total.astype(jnp.bfloat16)
                third_copy(k, my_high).start()

            @pl.when(k == high - 1)
            def _():
                red_ref[...] = total[:mode_rows]
                load_ref[...] = total[mode_rows:]

        return carry

    lax.fori_loop(0, high + 2, step_of, 0)

    def gathered(k, carry):
        slot = lax.rem(my_high + 1 + k, high)
        third_copy(k, slot).wait_recv()
        value = z_in[slot].astype(jnp.float32)
        red_ref[...] += value[:mode_rows]
        load_ref[...] += value[mode_rows:]
        third_copy(k, my_high).wait_send()
        return carry

    lax.fori_loop(0, high - 1, gathered, 0)

    def drained(k, carry):
        first_copy(k).wait_send()
        second_copy(k).wait_send()
        return carry

    lax.fori_loop(0, high, drained, 0)
    for step in range(1, n_panel):
        panel_copy(step, panel).wait_send()

    @pl.when(sub < n_sub - 1)
    def _():
        halo_copy(0).wait_send()

    @pl.when(sub > 0)
    def _():
        halo_copy(1).wait_send()


def body(
    n_sub,
    n_panel,
    stiffness_tiles,
    tile_columns,
    tile_counts,
    phi_modes,
    halo_to_right,
    halo_to_left,
    liner_rows,
    liner_owner,
    liner_slot,
):
    block_rows, slots, tile, _ = stiffness_tiles.shape
    rows, width = phi_modes.shape
    high = n_sub // LOW
    mode_rows = width * n_panel // n_sub
    out_rows = mode_rows + IF_DEV
    halo = halo_to_right.shape[0]
    listed = liner_rows.shape[0]
    target = (liner_owner[:, 0] * IF_DEV + liner_slot).reshape(1, listed)
    bf16, f32 = jnp.bfloat16, jnp.float32
    smem = pl.BlockSpec(memory_space=pltpu.SMEM)
    vmem = pl.BlockSpec(memory_space=pltpu.VMEM)
    hbm = pl.BlockSpec(memory_space=pl.ANY)
    dma = pltpu.SemaphoreType.DMA
    return pl.pallas_call(
        functools.partial(kernel, n_sub, n_panel),
        out_shape=(
            jax.ShapeDtypeStruct((mode_rows, width), f32),
            jax.ShapeDtypeStruct((IF_DEV, width), f32),
        ),
        in_specs=[smem, smem, smem, smem, vmem, vmem, hbm, hbm],
        out_specs=(vmem, vmem),
        scratch_shapes=[
            pltpu.VMEM((block_rows + 2 * halo, tile, width), bf16),
            pltpu.VMEM((block_rows, slots, tile, tile), bf16),
            pltpu.VMEM((rows, listed), bf16),
            pltpu.VMEM((high, LOW, out_rows, rows), bf16),
            pltpu.VMEM((rows, width), bf16),
            pltpu.VMEM((high, LOW, out_rows, width), f32),
            pltpu.VMEM((2, halo, tile, width), bf16),
            pltpu.VMEM((high, 2, out_rows, width), bf16),
            pltpu.VMEM((high, 2, out_rows, width), bf16),
            pltpu.VMEM((high, out_rows, width), bf16),
            pltpu.VMEM((high, out_rows, width), bf16),
            pltpu.VMEM((high, out_rows, width), bf16),
            pltpu.VMEM((high, out_rows, width), bf16),
            dma((2,)),
            dma((2,)),
            dma((2,)),
            dma((n_panel,)),
            dma((n_panel,)),
            dma((high,)),
            dma((high,)),
            dma((high,)),
            dma((high,)),
            dma((high,)),
            dma((high,)),
        ],
        compiler_params=pltpu.CompilerParams(
            collective_id=0, has_side_effects=True, vmem_limit_bytes=60 << 20
        ),
    )(
        tile_columns,
        tile_counts,
        halo_to_right,
        halo_to_left,
        liner_rows.reshape(1, listed),
        target,
        stiffness_tiles,
        phi_modes.reshape(block_rows, tile, width),
    )


def solution(mesh):
    return jax.shard_map(
        functools.partial(body, mesh.shape["sub"], mesh.shape["panel"]),
        mesh=mesh,
        in_specs=(
            P("sub", None, None, None),
            P("sub", None),
            P("sub", None),
            P("sub", "panel"),
            P("sub"),
            P("sub"),
            P("sub"),
            P("sub", None),
            P("sub"),
        ),
        out_specs=(P("sub", "panel"), P("sub", "panel")),
        check_vma=False,
    )
```

```python
import functools

import jax
import jax.numpy as jnp
from jax import lax
from jax.experimental import pallas as pl
from jax.experimental.pallas import tpu as pltpu
from jax.sharding import PartitionSpec as P

IF_DEV = 32
LOW = 4
PARTS = 2
MESH = pl.DeviceIdType.MESH


def kernel(
    n_sub,
    n_panel,
    cols_ref,
    counts_ref,
    to_right_ref,
    to_left_ref,
    rows_ref,
    target_ref,
    tiles_hbm,
    phi_hbm,
    red_ref,
    load_ref,
    ext,
    tiles,
    onehot,
    lhs,
    kphi,
    part,
    halo_out,
    halo_in,
    s1_out,
    s1_in,
    s2_out,
    s2_in,
    z_out,
    z_in,
    local_sem,
    halo_send,
    halo_recv,
    pan_send,
    pan_recv,
    s1_send,
    s1_recv,
    s2_send,
    s2_recv,
    z_send,
    z_recv,
):
    block_rows, slots, tile, _ = tiles.shape
    halo = halo_out.shape[2]
    rows = block_rows * tile
    width = kphi.shape[2]
    high = n_sub // LOW
    mode_rows = red_ref.shape[0]
    out_rows = mode_rows + IF_DEV
    per_panel = high // n_panel
    sub = lax.axis_index("sub")
    panel = lax.axis_index("panel")
    low, my_high = lax.rem(sub, LOW), sub // LOW
    bit0, bit1 = lax.rem(low, 2), low // 2

    def order(part_of):
        swap = 1 - part_of * (1 - lax.rem(panel, 2))
        first_bit = (1 - swap) * bit0 + swap * bit1
        second_bit = (1 - swap) * bit1 + swap * bit0
        first_weight, second_weight = 1 + swap, 2 - swap
        first_peer = sub + (1 - 2 * first_bit) * first_weight
        second_peer = sub + (1 - 2 * second_bit) * second_weight
        return first_bit, second_bit, first_weight, second_weight, first_peer, second_peer

    barrier = pltpu.get_barrier_semaphore()

    def greet(place):
        pl.semaphore_signal(barrier, inc=1, device_id=place, device_id_type=MESH)

    greet({"sub": sub + 1 - 2 * bit0, "panel": panel})
    greet({"sub": sub + 2 - 4 * bit1, "panel": panel})

    @pl.when(sub > 0)
    def _():
        greet({"sub": sub - 1, "panel": panel})

    @pl.when(sub < n_sub - 1)
    def _():
        greet({"sub": sub + 1, "panel": panel})

    for step in range(1, n_panel):
        greet({"sub": sub, "panel": lax.rem(panel + step, n_panel)})
    for step in range(1, high):
        greet({"sub": lax.rem(my_high + step, high) * LOW + low, "panel": panel})

    phi_copies = [
        pltpu.make_async_copy(
            phi_hbm.at[:, :, pl.ds(c * width, width)],
            ext.at[c, pl.ds(halo, block_rows)],
            local_sem.at[c],
        )
        for c in range(PARTS)
    ]
    tile_copy = pltpu.make_async_copy(tiles_hbm, tiles, local_sem.at[PARTS])
    for copy in phi_copies:
        copy.start()
    tile_copy.start()
    for copy in phi_copies:
        copy.wait()
    for c in range(PARTS):
        for i in range(halo):
            halo_out[c, 0, i] = ext[c, halo + to_right_ref[i]]
            halo_out[c, 1, i] = ext[c, halo + to_left_ref[i]]
    ends = jnp.where(sub > 0, 1, 0) + jnp.where(sub < n_sub - 1, 1, 0)
    pl.semaphore_wait(barrier, 2 + (n_panel - 1) + (high - 1) + ends)

    def halo_copy(c, side):
        return pltpu.make_async_remote_copy(
            src_ref=halo_out.at[c, side],
            dst_ref=halo_in.at[c, side],
            send_sem=halo_send.at[c, side],
            recv_sem=halo_recv.at[c, side],
            device_id={"sub": sub + 1 - 2 * side, "panel": panel},
            device_id_type=MESH,
        )

    def send_halo(c):
        @pl.when(sub < n_sub - 1)
        def _():
            halo_copy(c, 0).start()

        @pl.when(sub > 0)
        def _():
            halo_copy(c, 1).start()

    send_halo(0)

    def transposed(b, carry):
        for q in range(per_panel * LOW):
            lhs[
                panel * per_panel + q // LOW,
                q % LOW,
                pl.ds(0, mode_rows),
                pl.ds(pl.multiple_of(b * tile, tile), tile),
            ] = jnp.transpose(
                ext[
                    q * mode_rows // width,
                    halo + b,
                    :,
                    pl.ds(q * mode_rows % width, mode_rows),
                ]
            )
        return carry

    lax.fori_loop(0, block_rows, transposed, 0)

    def panel_copy(step, owner):
        block = lhs.at[
            pl.ds(owner * per_panel, per_panel), :, pl.ds(0, mode_rows), :
        ]
        return pltpu.make_async_remote_copy(
            src_ref=block,
            dst_ref=block,
            send_sem=pan_send.at[step],
            recv_sem=pan_recv.at[step],
            device_id={"sub": sub, "panel": lax.rem(panel + step, n_panel)},
            device_id_type=MESH,
        )

    for step in range(1, n_panel):
        panel_copy(step, panel).start()

    listed = rows_ref.shape[1]
    onehot[...] = (
        lax.broadcasted_iota(jnp.int32, (rows, listed), 0) == rows_ref[...]
    ).astype(jnp.float32).astype(jnp.bfloat16)
    wanted = LOW * IF_DEV

    def select(h, carry):
        place = lax.broadcasted_iota(jnp.int32, (wanted, listed), 0) + h * wanted
        hit = (place == target_ref[...]).astype(jnp.float32).astype(jnp.bfloat16)
        found = lax.dot_general(
            hit,
            onehot[...],
            (((1,), (1,)), ((), ())),
            preferred_element_type=jnp.float32,
        ).astype(jnp.bfloat16)
        for q in range(LOW):
            lhs[h, q, pl.ds(mode_rows, IF_DEV), :] = found[
                q * IF_DEV : (q + 1) * IF_DEV
            ]
        return carry

    lax.fori_loop(0, high, select, 0)
    tile_copy.wait()

    def products(c):
        for side in range(2):
            there = sub > 0 if side == 0 else sub < n_sub - 1
            place = pl.ds(side * (halo + block_rows), halo)

            @pl.when(there)
            def _(side=side, place=place):
                halo_copy(c, side).wait_recv()
                ext[c, place] = halo_in[c, side]

            @pl.when(jnp.logical_not(there))
            def _(place=place):
                ext[c, place] = jnp.zeros((halo, tile, width), ext.dtype)

        if c + 1 < PARTS:
            send_halo(c + 1)

        def block_row(b, carry):
            count = counts_ref[0, b]
            left = jnp.concatenate(
                [
                    jnp.where(j < count, tiles[b, j].astype(jnp.float32), 0.0).astype(
                        jnp.bfloat16
                    )
                    for j in range(slots)
                ],
                axis=1,
            )
            right = jnp.concatenate(
                [ext[c, cols_ref[j, b]] for j in range(slots)], axis=0
            )
            kphi[c, pl.ds(pl.multiple_of(b * tile, tile), tile), :] = jnp.dot(
                left, right, preferred_element_type=jnp.float32
            ).astype(jnp.bfloat16)
            return carry

        lax.fori_loop(0, block_rows, block_row, 0)

    products(0)

    for step in range(1, n_panel):
        panel_copy(step, lax.rem(panel + n_panel - step, n_panel)).wait_recv()

    def first_copy(k):
        return pltpu.make_async_remote_copy(
            src_ref=s1_out.at[k],
            dst_ref=s1_in.at[k],
            send_sem=s1_send.at[k],
            recv_sem=s1_recv.at[k],
            device_id={"sub": order(k // high)[4], "panel": panel},
            device_id_type=MESH,
        )

    def second_copy(k):
        return pltpu.make_async_remote_copy(
            src_ref=s2_out.at[k],
            dst_ref=s2_in.at[k],
            send_sem=s2_send.at[k],
            recv_sem=s2_recv.at[k],
            device_id={"sub": order(k // high)[5], "panel": panel},
            device_id_type=MESH,
        )

    def third_copy(k, slot):
        return pltpu.make_async_remote_copy(
            src_ref=z_out.at[k],
            dst_ref=z_in.at[slot],
            send_sem=z_send.at[k],
            recv_sem=z_recv.at[slot],
            device_id={
                "sub": lax.rem(my_high + 1 + lax.rem(k, high), high) * LOW + low,
                "panel": panel,
            },
            device_id_type=MESH,
        )

    chunk = min(256, width)

    total_steps = PARTS * high
    lag = 3

    def step_of(t, carry):
        for c in range(1, PARTS):

            @pl.when(t == c * high)
            def _(c=c):
                products(c)

        @pl.when(t < total_steps)
        def _():
            c = t // high
            h = lax.rem(my_high + 1 + lax.rem(t, high), high)
            first_bit, _, first_weight, second_weight, _, _ = order(c)

            def columns(i, inner):
                at = pl.ds(pl.multiple_of(i * chunk, chunk), chunk)
                product = jnp.dot(
                    lhs[h].reshape(LOW * out_rows, rows),
                    kphi[c, :, at],
                    preferred_element_type=jnp.float32,
                )
                part[t, :, :, at] = product.reshape(LOW, out_rows, chunk)
                return inner

            lax.fori_loop(0, width // chunk, columns, 0)
            for j in range(2):
                q = (1 - first_bit) * first_weight + j * second_weight
                s1_out[t, j] = part[t, q].astype(jnp.bfloat16)
            first_copy(t).start()

        @pl.when((t >= lag) & (t < total_steps + lag))
        def _():
            k = t - lag
            first_bit, second_bit, first_weight, second_weight, _, _ = order(k // high)
            first_copy(k).wait_recv()
            q = first_bit * first_weight + (1 - second_bit) * second_weight
            s2_out[k] = (
                part[k, q] + s1_in[k, 1 - second_bit].astype(jnp.float32)
            ).astype(jnp.bfloat16)
            second_copy(k).start()

        @pl.when(t >= lag + 1)
        def _():
            k = t - lag - 1
            _, second_bit, _, _, _, _ = order(k // high)
            second_copy(k).wait_recv()
            total = (
                part[k, low]
                + s1_in[k, second_bit].astype(jnp.float32)
                + s2_in[k].astype(jnp.float32)
            )

            @pl.when(lax.rem(k, high) < high - 1)
            def _():
                z_out[k] = total.astype(jnp.bfloat16)
                third_copy(k, k // high * high + my_high).start()

            for c in range(PARTS):

                @pl.when(k == (c + 1) * high - 1)
                def _(c=c):
                    red_ref[:, pl.ds(c * width, width)] = total[:mode_rows]
                    load_ref[:, pl.ds(c * width, width)] = total[mode_rows:]

        return carry

    lax.fori_loop(0, total_steps + lag + 1, step_of, 0)

    for c in range(PARTS):
        at_part = pl.ds(c * width, width)

        def gathered(k, carry, c=c, at_part=at_part):
            slot = c * high + lax.rem(my_high + 1 + k, high)
            third_copy(c * high + k, slot).wait_recv()
            value = z_in[slot].astype(jnp.float32)
            red_ref[:, at_part] += value[:mode_rows]
            load_ref[:, at_part] += value[mode_rows:]
            third_copy(c * high + k, slot).wait_send()
            return carry

        lax.fori_loop(0, high - 1, gathered, 0)

    def drained(k, carry):
        first_copy(k).wait_send()
        second_copy(k).wait_send()
        return carry

    lax.fori_loop(0, total_steps, drained, 0)
    for step in range(1, n_panel):
        panel_copy(step, panel).wait_send()

    for c in range(PARTS):

        @pl.when(sub < n_sub - 1)
        def _(c=c):
            halo_copy(c, 0).wait_send()

        @pl.when(sub > 0)
        def _(c=c):
            halo_copy(c, 1).wait_send()


def body(
    n_sub,
    n_panel,
    stiffness_tiles,
    tile_columns,
    tile_counts,
    phi_modes,
    halo_to_right,
    halo_to_left,
    liner_rows,
    liner_owner,
    liner_slot,
):
    block_rows, slots, tile, _ = stiffness_tiles.shape
    rows, width = phi_modes.shape
    high = n_sub // LOW
    mode_rows = width * n_panel // n_sub
    out_rows = mode_rows + IF_DEV
    halo = halo_to_right.shape[0]
    half = width // PARTS
    listed = liner_rows.shape[0]
    target = (liner_owner[:, 0] * IF_DEV + liner_slot).reshape(1, listed)
    bf16, f32 = jnp.bfloat16, jnp.float32
    smem = pl.BlockSpec(memory_space=pltpu.SMEM)
    vmem = pl.BlockSpec(memory_space=pltpu.VMEM)
    hbm = pl.BlockSpec(memory_space=pl.ANY)
    dma = pltpu.SemaphoreType.DMA
    return pl.pallas_call(
        functools.partial(kernel, n_sub, n_panel),
        out_shape=(
            jax.ShapeDtypeStruct((mode_rows, width), f32),
            jax.ShapeDtypeStruct((IF_DEV, width), f32),
        ),
        in_specs=[smem, smem, smem, smem, vmem, vmem, hbm, hbm],
        out_specs=(vmem, vmem),
        scratch_shapes=[
            pltpu.VMEM((PARTS, block_rows + 2 * halo, tile, half), bf16),
            pltpu.VMEM((block_rows, slots, tile, tile), bf16),
            pltpu.VMEM((rows, listed), bf16),
            pltpu.VMEM((high, LOW, out_rows, rows), bf16),
            pltpu.VMEM((PARTS, rows, half), bf16),
            pltpu.VMEM((PARTS * high, LOW, out_rows, half), f32),
            pltpu.VMEM((PARTS, 2, halo, tile, half), bf16),
            pltpu.VMEM((PARTS, 2, halo, tile, half), bf16),
            pltpu.VMEM((PARTS * high, 2, out_rows, half), bf16),
            pltpu.VMEM((PARTS * high, 2, out_rows, half), bf16),
            pltpu.VMEM((PARTS * high, out_rows, half), bf16),
            pltpu.VMEM((PARTS * high, out_rows, half), bf16),
            pltpu.VMEM((PARTS * high, out_rows, half), bf16),
            pltpu.VMEM((PARTS * high, out_rows, half), bf16),
            dma((PARTS + 1,)),
            dma((PARTS, 2)),
            dma((PARTS, 2)),
            dma((n_panel,)),
            dma((n_panel,)),
        ]
        + [dma((PARTS * high,))] * 6,
        compiler_params=pltpu.CompilerParams(
            collective_id=0, has_side_effects=True, vmem_limit_bytes=60 << 20
        ),
    )(
        tile_columns.T,
        tile_counts,
        halo_to_right,
        halo_to_left,
        liner_rows.reshape(1, listed),
        target,
        stiffness_tiles,
        phi_modes.reshape(block_rows, tile, width),
    )


def solution(mesh):
    return jax.shard_map(
        functools.partial(body, mesh.shape["sub"], mesh.shape["panel"]),
        mesh=mesh,
        in_specs=(
            P("sub", None, None, None),
            P("sub", None),
            P("sub", None),
            P("sub", "panel"),
            P("sub"),
            P("sub"),
            P("sub"),
            P("sub", None),
            P("sub"),
        ),
        out_specs=(P("sub", "panel"), P("sub", "panel")),
        check_vma=False,
    )
```
